32 devices in a mesh: grp: 4 (over y, core), in: 8 (over z, x).
Axes of the slice: x: 2, y: 2, z: 4, core: 2. Of those that a mesh axis runs over, the one named last changes fastest.
Arguments:
- tokens: bfloat16 [32, 144, 8192], P(('grp', 'in')), may hold values from -6 to 6
- queries: bfloat16 [32, 144, 1024], P(('grp', 'in')), may hold values from -120 to 120
- key_rows: bfloat16 [32, 144, 128], P(('grp', 'in')), may hold values from -5 to 5
- cotangent: bfloat16 [32, 144, 1024], P(('grp', 'in')), may hold values from -6 to 6
- segments: int32 [32, 144], P(('grp', 'in')), may hold values from 0 to 3, as said below
- levels: bfloat16 [64, 128, 128], P('in'), may hold values from -127 to 127, as said below
- scales: bfloat16 [64, 128], P('in'), may hold values from 4.9829483e-05 to 0.00049972534
Outputs:
- attended: bfloat16 [32, 144, 1024], P(('grp', 'in'))
- query_grad: bfloat16 [32, 144, 1024], P(('grp', 'in'))
- key_grad: bfloat16 [32, 144, 128], P(('grp', 'in'))
- value_weight_grad: float32 [128, 8192], P('grp', 'in')
The draws below stay inside these ranges and needn't reach their ends.
Inputs may be any that keep to these rules, and one draw needn't show every extreme that they name: `segments`: within each sequence the numbers never fall, start at 0, grow by one at each of 3 distinct positions, and the last two positions share a document. `levels`: whole numbers.
All inputs are finite; a program needn't handle non-finite values.
Results may differ from the reference program's by a relative error of at most 0.0085.
Values may be sent and summed in bfloat16 or wider, within the bound.
A program may use at most 64 MiB of HBM per device.

```python
import math
import jax
import jax.numpy as jnp
from jax import lax

D = 8192
HD = 128
HEADS = 8
QB = 128
SEG_CUTS = 3
TOK_DEV = 144
ROWS_N = 32
N_GRP = 4
N_IN = 8


def key_base(key):
    normal_rows = jax.random.normal(key, (ROWS_N, TOK_DEV, HD), jnp.float32)
    return jnp.clip(normal_rows, -5.0, 5.0)


def draw_key_rows(key, part):
    base_rows = key_base(key)
    return base_rows.astype(jnp.bfloat16)


def draw_queries(key, part):
    key = jax.random.fold_in(key, 5)
    drawn = jnp.clip(jax.random.normal(key, (ROWS_N, TOK_DEV, HEADS * HD), jnp.float32), -5.0, 5.0)
    return drawn.astype(jnp.bfloat16)


def draw_segments(key, part):
    key = jax.random.fold_in(key, 11)
    row_keys = jax.random.split(key, ROWS_N)

    def one_row(row_key):
        cuts = jax.random.permutation(row_key, TOK_DEV - 2)[:SEG_CUTS] + 1
        position = jnp.arange(TOK_DEV)
        return jnp.sum((position[:, None] >= cuts[None, :]).astype(jnp.int32), axis=1).astype(jnp.int32)
    return jax.vmap(one_row)(row_keys)


def draw_levels(key, part):
    key = jax.random.fold_in(key, 7)
    whole = jax.random.randint(key, (D // QB, QB, HD), -127, 128)
    return whole.astype(jnp.float32).astype(jnp.bfloat16)


def strengthened(result, own_key, source, target, shards_of, factor):
    def block_of(axis_at):
        return (jnp.arange(result.shape[axis_at]) // (result.shape[axis_at] // shards_of)).reshape((-1,) + (1,) * (result.ndim - 1 - axis_at))

    first = jax.random.permutation(own_key, shards_of)[block_of(target)]
    second = (block_of(target) + shards_of // 2) % shards_of
    return jnp.where((block_of(source) == first) | (block_of(source) == second), factor * result, result)


def shard_levels(rng, dims, cuts, least, top_value):
    level, own = 1.0, jax.random.fold_in(rng, 6)
    for axis_at, parts in cuts:
        draws = jnp.exp(jax.random.uniform(jax.random.fold_in(own, axis_at), (parts,), jnp.float32, least / len(cuts), top_value / len(cuts)))
        level = level * jnp.repeat(draws, dims[axis_at] // parts).reshape([-1 if axis == axis_at else 1 for axis in range(len(dims))])
    return level


def centred(key, shape, spread, limit, pieces=(), held_as=jnp.bfloat16):
    drawn = spread * jax.random.normal(key, shape, jnp.float32)
    if pieces:
        drawn = drawn * shard_levels(key, shape, pieces, -0.22, 0.18)
    return jnp.clip(drawn, -limit, limit).astype(held_as)


def heavy_noise(own_key, shape, scale, bound, cuts, heavy, kind=jnp.bfloat16):
    values = scale * jax.random.normal(own_key, shape, jnp.float32)
    if cuts:
        values = values * shard_levels(own_key, shape, cuts, -0.22, 0.18)
    return jnp.clip(strengthened(values, jax.random.fold_in(own_key, 3), *heavy), -bound, bound).astype(kind)


def setup_inputs(seed: int = 0) -> dict:
    streams_of = jax.random.split(jax.random.key(seed), 8)
    tokens = heavy_noise(streams_of[0], (ROWS_N, TOK_DEV, D), 1.0, 6.0, ((0, 32),), (0, 2, 32, 2.75))
    queries = draw_queries(jax.random.fold_in(streams_of[7], 71), 0)
    key_rows = draw_key_rows(jax.random.fold_in(streams_of[7], 71), 0)
    cotangent = centred(streams_of[3], (ROWS_N, TOK_DEV, HEADS * HD), 1.0, 6.0, ((0, 32),))
    segments = draw_segments(jax.random.fold_in(streams_of[7], 71), 0)
    levels = draw_levels(jax.random.fold_in(streams_of[7], 71), 0)
    scales = jnp.clip(jnp.exp(math.log(0.00049972534) - 2.3054518 * jax.random.uniform(streams_of[6], (D // QB, HD), jnp.float32) ** shard_levels(streams_of[6], (D // QB, HD), ((0, 8),), -0.2, 0.2)), 4.982948303222656e-05, 0.00049972534).astype(jnp.bfloat16)
    return dict(tokens=tokens, queries=queries, key_rows=key_rows, cotangent=cotangent, segments=segments, levels=levels, scales=scales)


def dequantize(levels, scales):
    blocks = levels.astype(jnp.float32) * scales.astype(jnp.float32)[:, None, :]
    return blocks.reshape(-1, blocks.shape[2]).astype(jnp.bfloat16)


def attend(tokens_one, queries_one, keys_one, cotangent_one, segments_one, weight):
    length = tokens_one.shape[0]
    head_size = keys_one.shape[1]
    factor = head_size ** -0.5
    values = jnp.dot(tokens_one, weight, preferred_element_type=jnp.float32).astype(jnp.bfloat16)
    query_heads = queries_one.reshape(length, HEADS, head_size)
    cot_heads = cotangent_one.reshape(length, HEADS, head_size)
    scores = jnp.einsum('sgd,td->gst', query_heads.astype(jnp.float32), keys_one.astype(jnp.float32)) * factor
    position = jnp.arange(length)
    allowed = (position[:, None] >= position[None, :]) & (segments_one[:, None] == segments_one[None, :])
    scores = jnp.where(allowed[None], scores, -jnp.inf)
    row_top = jnp.max(scores, axis=-1, keepdims=True)
    expo = jnp.exp(scores - row_top)
    probs = expo / jnp.sum(expo, axis=-1, keepdims=True)
    probs_low = probs.astype(jnp.bfloat16)
    attended = jnp.einsum('gst,td->sgd', probs_low.astype(jnp.float32), values.astype(jnp.float32))
    attended = attended.reshape(length, HEADS * head_size).astype(jnp.bfloat16)
    value_grad = jnp.einsum('gst,sgd->td', probs_low.astype(jnp.float32), cot_heads.astype(jnp.float32)).astype(jnp.bfloat16)
    prob_grad = jnp.einsum('sgd,td->gst', cot_heads.astype(jnp.float32), values.astype(jnp.float32))
    centre = jnp.sum(probs * prob_grad, axis=-1, keepdims=True)
    score_grad = (probs * (prob_grad - centre) * factor).astype(jnp.bfloat16)
    query_grad = jnp.einsum('gst,td->sgd', score_grad.astype(jnp.float32), keys_one.astype(jnp.float32))
    query_grad = query_grad.reshape(length, HEADS * head_size).astype(jnp.bfloat16)
    key_grad = jnp.einsum('gst,sgd->td', score_grad.astype(jnp.float32), query_heads.astype(jnp.float32)).astype(jnp.bfloat16)
    term = jnp.dot(value_grad.T, tokens_one, preferred_element_type=jnp.float32).astype(jnp.bfloat16)
    return attended, query_grad, key_grad, term


def reference(tokens, queries, key_rows, cotangent, segments, levels, scales):
    weight = dequantize(levels, scales)
    width = tokens.shape[2]
    head_size = key_rows.shape[2]

    def split(array):
        return array.reshape((N_GRP, N_IN) + array.shape[1:])

    inputs = (split(tokens), split(queries), split(key_rows), split(cotangent), split(segments))

    def group_step(total, group_items):
        def member_step(partial_sum, item):
            attended, query_grad, key_grad, term = attend(item[0], item[1], item[2], item[3], item[4], weight)
            return partial_sum + term.astype(jnp.float32), (attended, query_grad, key_grad)

        start = jnp.zeros((head_size, width), jnp.float32)
        group_total, outputs = lax.scan(member_step, start, group_items)
        return total + group_total.astype(jnp.bfloat16).astype(jnp.float32), outputs

    initial = jnp.zeros((head_size, width), jnp.float32)
    total, outputs = lax.scan(group_step, initial, inputs)
    attended = outputs[0].reshape((ROWS_N,) + outputs[0].shape[2:])
    query_grad = outputs[1].reshape((ROWS_N,) + outputs[1].shape[2:])
    key_grad = outputs[2].reshape((ROWS_N,) + outputs[2].shape[2:])
    return attended, query_grad, key_grad, total / ROWS_N
```

```python
import functools
import math

import jax
import jax.numpy as jnp
from jax import lax
from jax.experimental import pallas as pl
from jax.experimental.pallas import tpu as pltpu
from jax.sharding import PartitionSpec as P

MESH = pl.DeviceIdType.MESH
F32 = jnp.float32
BF16 = jnp.bfloat16


def dot(a, b, ca, cb):
    return lax.dot_general(a, b, (((ca,), (cb,)), ((), ())), preferred_element_type=F32)


def remote(src, dst, send, recv, dev):
    return pltpu.make_async_remote_copy(
        src_ref=src, dst_ref=dst, send_sem=send, recv_sem=recv, device_id=dev, device_id_type=MESH
    )


def kernel(
    dims,
    tok_hbm, q_hbm, k_ref, cot_hbm, seg_ref, lev_hbm, sca_ref,
    att_hbm, qg_hbm, kg_hbm, wg_hbm,
    tok, qs, cs, lev, wbuf, probs, probs_low, sg_low,
    term_send, term_own, term_recv, sum_core, y_recv, sum_y, x_recv, sum_x, z_recv,
    att_v, qg_v, kg_v, wg_v,
    in_sem, q_sem, c_sem, out_sem,
    core_s, core_r, ys_s, ys_r, xs_s, xs_r, zs_s, zs_r,
    gz_s, gz_r, gx_s, gx_r, gc_s, gc_r,
):
    Y, X, Z, heads, L, hd = dims
    r, c_w = wg_v.shape
    g, i = lax.axis_index("grp"), lax.axis_index("in")
    y, c = g // 2, lax.rem(g, 2)
    z, x = i // X, lax.rem(i, X)
    other = 1 - c
    core_dev = (y * 2 + other, i)

    def y_dev(d):
        return (lax.rem(y + d, Y) * 2 + c, i)

    def x_dev(d):
        return (g, z * X + lax.rem(x + d, X))

    def z_dev(d):
        return (g, lax.rem(z + d, Z) * X + x)

    lev_cp = pltpu.make_async_copy(lev_hbm, lev, in_sem.at[0])
    lev_cp.start()
    q_cps, c_cps = [], []
    for h in range(heads):
        q_cps.append(pltpu.make_async_copy(
            q_hbm.at[0, :, pl.ds(h * hd, hd)], qs.at[pl.ds(h * L, L)], q_sem.at[h]))
        q_cps[-1].start()
    for h in range(heads):
        c_cps.append(pltpu.make_async_copy(
            cot_hbm.at[0, :, pl.ds(h * hd, hd)], cs.at[pl.ds(h * L, L)], c_sem.at[h]))
        c_cps[-1].start()
    tok_cp = pltpu.make_async_copy(tok_hbm.at[0], tok, in_sem.at[1])
    tok_cp.start()

    barrier = pltpu.get_barrier_semaphore()
    peers = [core_dev]
    peers += [y_dev(d) for d in range(1, Y)]
    peers += [x_dev(d) for d in range(1, X)]
    peers += [z_dev(d) for d in range(1, Z)]
    for dev in peers:
        pl.semaphore_signal(barrier, inc=1, device_id=dev, device_id_type=MESH)

    lev_cp.wait()
    blocks, block_rows = lev.shape[0], lev.shape[1]
    sca = sca_ref[...].astype(F32)
    if blocks > 1:
        hb = blocks // 2
        s_half = jnp.where(c == 0, sca[:hb], sca[hb:])
        own_w = lev[pl.ds(c * hb, hb)].astype(F32) * s_half[:, None, :]
        own_w = own_w.reshape(hb * block_rows, hd)
    else:
        hr = block_rows // 2
        own_w = lev[0, pl.ds(pl.multiple_of(c * hr, hr), hr)].astype(F32) * sca
    wbuf[i, c] = own_w.astype(BF16)

    pl.semaphore_wait(barrier, len(peers))

    sends = []

    def start(cp):
        cp.start()
        sends.append(cp)

    def piece(d, e):
        return lax.rem(z + Z - d, Z) * X + lax.rem(x + X - e, X)

    def forward_core(d, e):
        p = piece(d, e)
        start(remote(wbuf.at[p, c], wbuf.at[p, c], gc_s.at[d, e], gc_r.at[d, e], core_dev))

    def forward_x(d):
        p = piece(d, 0)
        for e in range(1, X):
            start(remote(wbuf.at[p, c], wbuf.at[p, c], gx_s.at[d, e], gx_r.at[d, e], x_dev(e)))

    def wait_z(d):
        p = piece(d, 0)
        remote(wbuf.at[p, c], wbuf.at[p, c], gz_s.at[d], gz_r.at[d], z_dev(d)).wait_recv()

    def wait_x(d, e):
        p = piece(d, e)
        remote(wbuf.at[p, c], wbuf.at[p, c], gx_s.at[d, e], gx_r.at[d, e], x_dev(e)).wait_recv()

    def wait_core(d, e):
        p = piece(d, e)
        remote(wbuf.at[p, other], wbuf.at[p, other], gc_s.at[d, e], gc_r.at[d, e], core_dev).wait_recv()

    for d in range(1, Z):
        start(remote(wbuf.at[i, c], wbuf.at[i, c], gz_s.at[d], gz_r.at[d], z_dev(d)))
    forward_x(0)
    forward_core(0, 0)

    wide = heads * L
    factor = hd ** -0.5
    keys = k_ref[0]
    lane = lax.broadcasted_iota(jnp.int32, (1, wide), 1)
    s_pos = lane
    for h in range(1, heads):
        s_pos = jnp.where(lane >= h * L, lane - h * L, s_pos)
    t_pos = lax.broadcasted_iota(jnp.int32, (L, 1), 0)
    seg_row = seg_ref[...].astype(F32)
    sq_r = lax.broadcasted_iota(jnp.int32, (L, L), 0)
    sq_c = lax.broadcasted_iota(jnp.int32, (L, L), 1)
    seg_col = jnp.sum(jnp.where(sq_r == sq_c, seg_row, 0.0), axis=1, keepdims=True)
    seg_wide = jnp.sum(jnp.where(t_pos == s_pos, seg_col, 0.0), axis=0, keepdims=True)
    allowed = (t_pos <= s_pos) & (seg_col == seg_wide)
    for cp in q_cps:
        cp.wait()
    scores = jnp.where(allowed, dot(keys, qs[...], 1, 1) * factor, -jnp.inf)
    expo = jnp.exp(scores - jnp.max(scores, axis=0, keepdims=True))
    pr = expo * (1.0 / jnp.sum(expo, axis=0, keepdims=True))
    probs[...] = pr
    probs_low[...] = pr.astype(BF16)
    for cp in c_cps:
        cp.wait()
    vg = dot(probs_low[...], cs[...], 1, 0).astype(BF16).astype(F32)
    vg_t = vg.T.reshape(Y, 2, r, L)
    mine = jnp.where(c == 0, vg_t[:, 0], vg_t[:, 1]).reshape(Y * r, L)
    theirs = jnp.where(c == 0, vg_t[:, 1], vg_t[:, 0]).reshape(Y * r, L)
    vg_rows = jnp.concatenate([theirs, mine], axis=0).astype(BF16)

    tok_cp.wait()
    half = Y * r
    for zz in range(Z):
        for xx in range(X):
            at = (zz * X + xx) * c_w
            t = dot(vg_rows, tok[:, at:at + c_w], 1, 0)
            term_send[zz, :, xx] = t[:half].reshape(Y, r, c_w).astype(BF16)
            term_own[zz, :, xx] = t[half:].reshape(Y, r, c_w)
        start(remote(term_send.at[zz], term_recv.at[zz], core_s.at[zz], core_r.at[zz], core_dev))

    for zz in range(Z):
        remote(term_send.at[zz], term_recv.at[zz], core_s.at[zz], core_r.at[zz], core_dev).wait_recv()
        sum_core[zz] = (term_own[zz] + term_recv[zz].astype(F32)).astype(BF16)
        for d in range(1, Y):
            start(remote(sum_core.at[zz, lax.rem(y + d, Y)], y_recv.at[zz, d],
                         ys_s.at[zz, d], ys_r.at[zz, d], y_dev(d)))

    for zz in range(Z):
        total = sum_core[zz, y].astype(F32)
        for d in range(1, Y):
            remote(y_recv.at[zz, d], y_recv.at[zz, d], ys_s.at[zz, d], ys_r.at[zz, d], y_dev(d)).wait_recv()
            total = total + y_recv[zz, d].astype(F32)
        sum_y[zz] = total.astype(BF16)
        for d in range(1, X):
            start(remote(sum_y.at[zz, lax.rem(x + d, X)], x_recv.at[zz, d],
                         xs_s.at[zz, d], xs_r.at[zz, d], x_dev(d)))
        if zz + 1 < Z:
            wait_z(zz + 1)
            forward_x(zz + 1)
            forward_core(zz + 1, 0)

    for zz in range(Z):
        total = sum_y[zz, x].astype(F32)
        for d in range(1, X):
            remote(x_recv.at[zz, d], x_recv.at[zz, d], xs_s.at[zz, d], xs_r.at[zz, d], x_dev(d)).wait_recv()
            total = total + x_recv[zz, d].astype(F32)
        sum_x[zz] = total.astype(BF16)
    for d in range(1, Z):
        start(remote(sum_x.at[lax.rem(z + d, Z)], z_recv.at[d], zs_s.at[d], zs_r.at[d], z_dev(d)))

    values = jnp.zeros((L, hd), F32)
    piece_rows = 2 * wbuf.shape[2]
    for d in range(Z):
        for e in range(1, X):
            wait_x(d, e)
            forward_core(d, e)
        if d:
            for e in range(X):
                wait_core(d - 1, e)
                p = piece(d - 1, e)
                cols = pl.ds(pl.multiple_of(p * piece_rows, 128), piece_rows)
                values = values + dot(tok[:, cols], wbuf[p].reshape(piece_rows, hd), 1, 0)
    for e in range(X):
        wait_core(Z - 1, e)
        p = piece(Z - 1, e)
        cols = pl.ds(pl.multiple_of(p * piece_rows, 128), piece_rows)
        values = values + dot(tok[:, cols], wbuf[p].reshape(piece_rows, hd), 1, 0)
    v_low = values.astype(BF16)

    outs = []
    att = dot(probs_low[...], v_low, 0, 0).astype(BF16)
    for h in range(heads):
        att_v[:, h * hd:(h + 1) * hd] = att[h * L:(h + 1) * L]
    outs.append(pltpu.make_async_copy(att_v, att_hbm.at[0], out_sem.at[0]))
    outs[-1].start()
    pg = dot(v_low, cs[...], 1, 1)
    weighted = probs[...] * pg
    centre = jnp.sum(weighted, axis=0, keepdims=True)
    sg_low[...] = ((weighted - probs[...] * centre) * factor).astype(BF16)
    qg = dot(sg_low[...], keys, 0, 0).astype(BF16)
    for h in range(heads):
        qg_v[:, h * hd:(h + 1) * hd] = qg[h * L:(h + 1) * L]
    outs.append(pltpu.make_async_copy(qg_v, qg_hbm.at[0], out_sem.at[1]))
    outs[-1].start()
    kg_v[...] = dot(sg_low[...], qs[...], 1, 0).astype(BF16)
    outs.append(pltpu.make_async_copy(kg_v, kg_hbm.at[0], out_sem.at[2]))
    outs[-1].start()

    total = sum_x[z].astype(F32)
    for d in range(1, Z):
        remote(z_recv.at[d], z_recv.at[d], zs_s.at[d], zs_r.at[d], z_dev(d)).wait_recv()
        total = total + z_recv[d].astype(F32)
    wg_v[...] = total * (1.0 / (2 * Y * X * Z))
    outs.append(pltpu.make_async_copy(wg_v, wg_hbm, out_sem.at[3]))
    outs[-1].start()
    for cp in sends:
        cp.wait_send()
    for cp in outs:
        cp.wait()


def solution(mesh):
    n_grp, n_in = mesh.shape["grp"], mesh.shape["in"]
    Y = n_grp // 2
    X = 2 ** (int(math.log2(n_in)) // 3)
    Z = n_in // X

    def step(tokens, queries, key_rows, cotangent, segments, levels, scales):
        _, L, D = tokens.shape
        hd = key_rows.shape[2]
        heads = queries.shape[2] // hd
        wide = heads * L
        r, c_w = hd // n_grp, D // n_in
        half_rows = c_w // 2
        any_spec = pl.BlockSpec(memory_space=pl.ANY)
        vmem = pl.BlockSpec(memory_space=pltpu.VMEM)
        DMA = pltpu.SemaphoreType.DMA
        return pl.pallas_call(
            functools.partial(kernel, (Y, X, Z, heads, L, hd)),
            out_shape=(
                jax.ShapeDtypeStruct(queries.shape, BF16),
                jax.ShapeDtypeStruct(queries.shape, BF16),
                jax.ShapeDtypeStruct(key_rows.shape, BF16),
                jax.ShapeDtypeStruct((r, c_w), F32),
            ),
            in_specs=[any_spec, any_spec, vmem, any_spec, vmem, any_spec, vmem],
            out_specs=(any_spec,) * 4,
            scratch_shapes=[
                pltpu.VMEM((L, D), BF16),
                pltpu.VMEM((wide, hd), BF16),
                pltpu.VMEM((wide, hd), BF16),
                pltpu.VMEM(levels.shape, BF16),
                pltpu.VMEM((n_in, 2, half_rows, hd), BF16),
                pltpu.VMEM((L, wide), F32),
                pltpu.VMEM((L, wide), BF16),
                pltpu.VMEM((L, wide), BF16),
                pltpu.VMEM((Z, Y, X, r, c_w), BF16),
                pltpu.VMEM((Z, Y, X, r, c_w), F32),
                pltpu.VMEM((Z, Y, X, r, c_w), BF16),
                pltpu.VMEM((Z, Y, X, r, c_w), BF16),
                pltpu.VMEM((Z, Y, X, r, c_w), BF16),
                pltpu.VMEM((Z, X, r, c_w), BF16),
                pltpu.VMEM((Z, X, r, c_w), BF16),
                pltpu.VMEM((Z, r, c_w), BF16),
                pltpu.VMEM((Z, r, c_w), BF16),
                pltpu.VMEM((L, heads * hd), BF16),
                pltpu.VMEM((L, heads * hd), BF16),
                pltpu.VMEM((L, hd), BF16),
                pltpu.VMEM((r, c_w), F32),
                DMA((2,)), DMA((heads,)), DMA((heads,)), DMA((4,)),
                DMA((Z,)), DMA((Z,)),
                DMA((Z, Y)), DMA((Z, Y)),
                DMA((Z, X)), DMA((Z, X)),
                DMA((Z,)), DMA((Z,)),
                DMA((Z,)), DMA((Z,)),
                DMA((Z, X)), DMA((Z, X)),
                DMA((Z, X)), DMA((Z, X)),
            ],
            compiler_params=pltpu.CompilerParams(
                collective_id=0, has_side_effects=True, vmem_limit_bytes=40 * 1024 * 1024
            ),
            cost_estimate=pl.CostEstimate(
                flops=2 * L * D * hd * 2 + 12 * heads * L * L * hd,
                bytes_accessed=8_000_000, transcendentals=heads * L * L,
            ),
        )(tokens, queries, key_rows, cotangent, segments, levels, scales)

    three = P(("grp", "in"), None, None)
    return jax.shard_map(
        step,
        mesh=mesh,
        in_specs=(three, three, three, three, P(("grp", "in"), None), P("in", None, None), P("in", None)),
        out_specs=(three, three, three, P("grp", "in")),
        check_vma=False,
    )
```

```python
import functools
import math

import jax
import jax.numpy as jnp
from jax import lax
from jax.experimental import pallas as pl
from jax.experimental.pallas import tpu as pltpu
from jax.sharding import PartitionSpec as P

MESH = pl.DeviceIdType.MESH
F32 = jnp.float32
BF16 = jnp.bfloat16


def dot(a, b, ca, cb):
    return lax.dot_general(a, b, (((ca,), (cb,)), ((), ())), preferred_element_type=F32)


def remote(src, dst, send, recv, dev):
    return pltpu.make_async_remote_copy(
        src_ref=src, dst_ref=dst, send_sem=send, recv_sem=recv, device_id=dev, device_id_type=MESH
    )


def kernel(
    dims,
    tok_hbm, q_hbm, k_hbm, cot_hbm, seg_hbm, lev_hbm, sca_hbm,
    att_hbm, qg_hbm, kg_hbm, wg_hbm,
    att_v, qg_v, kg_v, wg_v, key_v, seg_v, sca_v, tok, qs, cs, lev, wbuf, probs, probs_low, sg_low,
    term_send, term_own, term_recv, sum_core,
    ya_recv, xb_recv, sum_a, sum_b, xa_recv, yb_recv, sum_z, z_recv,
    in_sem, q_sem, c_sem, out_sem,
    core_s, core_r, ys_s, ys_r, xs_s, xs_r, zs_s, zs_r,
    gz_s, gz_r, gx_s, gx_r, gc_s, gc_r,
):
    Y, X, Z, heads, L, hd = dims
    r, c_w = wg_v.shape
    g, i = lax.axis_index("grp"), lax.axis_index("in")
    y, c = g // 2, lax.rem(g, 2)
    z, x = i // X, lax.rem(i, X)
    other = 1 - c
    core_dev = (y * 2 + other, i)

    def y_dev(d):
        return (lax.rem(y + d, Y) * 2 + c, i)

    def x_dev(d):
        return (g, z * X + lax.rem(x + d, X))

    def z_dev(d):
        return (g, lax.rem(z + d, Z) * X + x)

    lev_cp = pltpu.make_async_copy(lev_hbm, lev, in_sem.at[0])
    lev_cp.start()
    sca_cp = pltpu.make_async_copy(sca_hbm, sca_v, in_sem.at[2])
    sca_cp.start()
    key_cp = pltpu.make_async_copy(k_hbm.at[0], key_v, in_sem.at[3])
    key_cp.start()
    seg_cp = pltpu.make_async_copy(seg_hbm, seg_v, in_sem.at[4])
    seg_cp.start()
    q_cps, c_cps = [], []
    for h in range(heads):
        q_cps.append(pltpu.make_async_copy(
            q_hbm.at[0, :, pl.ds(h * hd, hd)], qs.at[pl.ds(h * L, L)], q_sem.at[h]))
        q_cps[-1].start()
    for h in range(heads):
        c_cps.append(pltpu.make_async_copy(
            cot_hbm.at[0, :, pl.ds(h * hd, hd)], cs.at[pl.ds(h * L, L)], c_sem.at[h]))
        c_cps[-1].start()
    tok_cp = pltpu.make_async_copy(tok_hbm.at[0], tok, in_sem.at[1])
    tok_cp.start()

    barrier = pltpu.get_barrier_semaphore()
    peers = [core_dev]
    peers += [y_dev(d) for d in range(1, Y)]
    peers += [x_dev(d) for d in range(1, X)]
    peers += [z_dev(d) for d in range(1, Z)]
    for dev in peers:
        pl.semaphore_signal(barrier, inc=1, device_id=dev, device_id_type=MESH)

    lev_cp.wait()
    blocks, block_rows = lev.shape[0], lev.shape[1]
    sca_cp.wait()
    sca = sca_v[...].astype(F32)
    if blocks > 1:
        hb = blocks // 2
        s_half = jnp.where(c == 0, sca[:hb], sca[hb:])
        own_w = lev[pl.ds(c * hb, hb)].astype(F32) * s_half[:, None, :]
        own_w = own_w.reshape(hb * block_rows, hd)
    else:
        hr = block_rows // 2
        own_w = lev[0, pl.ds(pl.multiple_of(c * hr, hr), hr)].astype(F32) * sca
    wbuf[i, c] = own_w.astype(BF16)

    pl.semaphore_wait(barrier, len(peers))

    sends = []
    outs = []

    def out(src, dst, k):
        outs.append(pltpu.make_async_copy(src, dst, out_sem.at[k]))
        outs[-1].start()

    def start(cp):
        cp.start()
        sends.append(cp)

    def piece(d, e):
        return lax.rem(z + Z - d, Z) * X + lax.rem(x + X - e, X)

    def forward_core(d, e):
        p = piece(d, e)
        start(remote(wbuf.at[p, c], wbuf.at[p, c], gc_s.at[d, e], gc_r.at[d, e], core_dev))

    def forward_x(d):
        p = piece(d, 0)
        for e in range(1, X):
            start(remote(wbuf.at[p, c], wbuf.at[p, c], gx_s.at[d, e], gx_r.at[d, e], x_dev(e)))

    def wait_z(d):
        p = piece(d, 0)
        remote(wbuf.at[p, c], wbuf.at[p, c], gz_s.at[d], gz_r.at[d], z_dev(d)).wait_recv()

    def wait_x(d, e):
        p = piece(d, e)
        remote(wbuf.at[p, c], wbuf.at[p, c], gx_s.at[d, e], gx_r.at[d, e], x_dev(e)).wait_recv()

    def wait_core(d, e):
        p = piece(d, e)
        remote(wbuf.at[p, other], wbuf.at[p, other], gc_s.at[d, e], gc_r.at[d, e], core_dev).wait_recv()

    for d in range(1, Z):
        start(remote(wbuf.at[i, c], wbuf.at[i, c], gz_s.at[d], gz_r.at[d], z_dev(d)))
    forward_x(0)
    forward_core(0, 0)

    wide = heads * L
    factor = hd ** -0.5
    key_cp.wait()
    seg_cp.wait()
    keys = key_v[...]
    lane = lax.broadcasted_iota(jnp.int32, (1, wide), 1)
    s_pos = lane
    for h in range(1, heads):
        s_pos = jnp.where(lane >= h * L, lane - h * L, s_pos)
    t_pos = lax.broadcasted_iota(jnp.int32, (L, 1), 0)
    seg_row = seg_v[...].astype(F32)
    sq_r = lax.broadcasted_iota(jnp.int32, (L, L), 0)
    sq_c = lax.broadcasted_iota(jnp.int32, (L, L), 1)
    seg_col = jnp.sum(jnp.where(sq_r == sq_c, seg_row, 0.0), axis=1, keepdims=True)
    seg_wide = jnp.sum(jnp.where(t_pos == s_pos, seg_col, 0.0), axis=0, keepdims=True)
    allowed = (t_pos <= s_pos) & (seg_col == seg_wide)
    for cp in q_cps:
        cp.wait()
    scores = jnp.where(allowed, dot(keys, qs[...], 1, 1) * factor, -jnp.inf)
    expo = jnp.exp(scores - jnp.max(scores, axis=0, keepdims=True))
    pr = expo * (1.0 / jnp.sum(expo, axis=0, keepdims=True))
    probs[...] = pr
    probs_low[...] = pr.astype(BF16)
    for cp in c_cps:
        cp.wait()
    vg = dot(probs_low[...], cs[...], 1, 0).astype(BF16).astype(F32)
    vg_t = vg.T.reshape(Y, 2, r, L)
    mine = jnp.where(c == 0, vg_t[:, 0], vg_t[:, 1]).reshape(Y * r, L)
    theirs = jnp.where(c == 0, vg_t[:, 1], vg_t[:, 0]).reshape(Y * r, L)
    vg_rows = jnp.concatenate([theirs, mine], axis=0).astype(BF16)

    tok_cp.wait()
    half = Y * r
    z_half = (Z + 1) // 2
    order = [zz for k in range(z_half) for zz in (k, k + z_half) if zz < Z]

    def y_copy(zz, d):
        if zz < z_half:
            src, dst = sum_core.at[zz, lax.rem(y + d, Y)], ya_recv.at[zz, d]
        else:
            src, dst = sum_b.at[zz, lax.rem(y + d, Y)], yb_recv.at[zz, d]
        return remote(src, dst, ys_s.at[zz, d], ys_r.at[zz, d], y_dev(d))

    def x_copy(zz, d):
        if zz < z_half:
            src, dst = sum_a.at[zz, lax.rem(x + d, X)], xa_recv.at[zz, d]
        else:
            src, dst = sum_core.at[zz, :, lax.rem(x + d, X)], xb_recv.at[zz, d]
        return remote(src, dst, xs_s.at[zz, d], xs_r.at[zz, d], x_dev(d))

    def core_copy(zz):
        return remote(term_send.at[zz], term_recv.at[zz], core_s.at[zz], core_r.at[zz], core_dev)

    for zz in order:
        for xx in range(X):
            at = (zz * X + xx) * c_w
            t = dot(vg_rows, tok[:, at:at + c_w], 1, 0)
            term_send[zz, :, xx] = t[:half].reshape(Y, r, c_w).astype(BF16)
            term_own[zz, :, xx] = t[half:].reshape(Y, r, c_w)
        start(core_copy(zz))

    for zz in order:
        core_copy(zz).wait_recv()
        sum_core[zz] = (term_own[zz] + term_recv[zz].astype(F32)).astype(BF16)
        for d in range(1, Y if zz < z_half else X):
            start(y_copy(zz, d) if zz < z_half else x_copy(zz, d))

    gathered = 0
    for zz in order:
        if zz < z_half:
            total = sum_core[zz, y].astype(F32)
            for d in range(1, Y):
                y_copy(zz, d).wait_recv()
                total = total + ya_recv[zz, d].astype(F32)
            sum_a[zz] = total.astype(BF16)
            for d in range(1, X):
                start(x_copy(zz, d))
        else:
            total = sum_core[zz, :, x].astype(F32)
            for d in range(1, X):
                x_copy(zz, d).wait_recv()
                total = total + xb_recv[zz, d].astype(F32)
            sum_b[zz] = total.astype(BF16)
            for d in range(1, Y):
                start(y_copy(zz, d))
        gathered += 1
        if gathered < Z:
            wait_z(gathered)
            forward_x(gathered)
            forward_core(gathered, 0)

    for zz in order:
        if zz < z_half:
            total = sum_a[zz, x].astype(F32)
            for d in range(1, X):
                x_copy(zz, d).wait_recv()
                total = total + xa_recv[zz, d].astype(F32)
        else:
            total = sum_b[zz, y].astype(F32)
            for d in range(1, Y):
                y_copy(zz, d).wait_recv()
                total = total + yb_recv[zz, d].astype(F32)
        sum_z[zz] = total.astype(BF16)

        @pl.when(z != zz)
        def _():
            d = lax.rem(zz + Z - z, Z)
            remote(sum_z.at[zz], z_recv.at[d], zs_s.at[d], zs_r.at[d], z_dev(d)).start()

    values = jnp.zeros((L, hd), F32)
    piece_rows = 2 * wbuf.shape[2]
    for d in range(Z):
        for e in range(1, X):
            wait_x(d, e)
            forward_core(d, e)
        if d:
            for e in range(X):
                wait_core(d - 1, e)
                p = piece(d - 1, e)
                cols = pl.ds(pl.multiple_of(p * piece_rows, 128), piece_rows)
                values = values + dot(tok[:, cols], wbuf[p].reshape(piece_rows, hd), 1, 0)
    for e in range(X):
        wait_core(Z - 1, e)
        p = piece(Z - 1, e)
        cols = pl.ds(pl.multiple_of(p * piece_rows, 128), piece_rows)
        values = values + dot(tok[:, cols], wbuf[p].reshape(piece_rows, hd), 1, 0)
    v_low = values.astype(BF16)

    att = dot(probs_low[...], v_low, 0, 0).astype(BF16)
    for h in range(heads):
        att_v[:, h * hd:(h + 1) * hd] = att[h * L:(h + 1) * L]
    out(att_v, att_hbm.at[0], 0)
    pg = dot(v_low, cs[...], 1, 1)
    weighted = probs[...] * pg
    centre = jnp.sum(weighted, axis=0, keepdims=True)
    sg_low[...] = ((weighted - probs[...] * centre) * factor).astype(BF16)
    qg = dot(sg_low[...], keys, 0, 0).astype(BF16)
    for h in range(heads):
        qg_v[:, h * hd:(h + 1) * hd] = qg[h * L:(h + 1) * L]
    out(qg_v, qg_hbm.at[0], 1)
    kg_v[...] = dot(sg_low[...], qs[...], 1, 0).astype(BF16)
    out(kg_v, kg_hbm.at[0], 2)

    total = sum_z[z].astype(F32)
    for d in range(1, Z):
        remote(z_recv.at[d], z_recv.at[d], zs_s.at[d], zs_r.at[d], z_dev(d)).wait_recv()
        total = total + z_recv[d].astype(F32)
    wg_v[...] = total * (1.0 / (2 * Y * X * Z))
    out(wg_v, wg_hbm, 3)
    for cp in sends:
        cp.wait_send()
    for d in range(1, Z):
        remote(sum_z.at[0], z_recv.at[d], zs_s.at[d], zs_r.at[d], z_dev(d)).wait_send()
    for cp in outs:
        cp.wait()


def write_out(*refs):
    held, sems = refs[8:12], refs[12]
    into = [pltpu.make_async_copy(refs[k], held[k], sems.at[k]) for k in range(4)]
    away = [pltpu.make_async_copy(held[k], refs[4 + k], sems.at[4 + k]) for k in range(4)]
    for cp in into:
        cp.start()
    for a, b in zip(into, away):
        a.wait()
        b.start()
    for cp in away:
        cp.wait()


def solution(mesh):
    n_grp, n_in = mesh.shape["grp"], mesh.shape["in"]
    Y = n_grp // 2
    X = 2 ** (int(math.log2(n_in)) // 3)
    Z = n_in // X

    def step(tokens, queries, key_rows, cotangent, segments, levels, scales):
        _, L, D = tokens.shape
        hd = key_rows.shape[2]
        heads = queries.shape[2] // hd
        wide = heads * L
        r, c_w = hd // n_grp, D // n_in
        half_rows = c_w // 2
        hbm = pl.BlockSpec(memory_space=pltpu.HBM)
        DMA = pltpu.SemaphoreType.DMA
        results = pl.pallas_call(
            functools.partial(kernel, (Y, X, Z, heads, L, hd)),
            out_shape=(
                jax.ShapeDtypeStruct(queries.shape, BF16),
                jax.ShapeDtypeStruct(queries.shape, BF16),
                jax.ShapeDtypeStruct(key_rows.shape, BF16),
                jax.ShapeDtypeStruct((r, c_w), F32),
            ),
            in_specs=[hbm] * 7,
            out_specs=(hbm,) * 4,
            scratch_shapes=[
                pltpu.VMEM((L, heads * hd), BF16),
                pltpu.VMEM((L, heads * hd), BF16),
                pltpu.VMEM((L, hd), BF16),
                pltpu.VMEM((r, c_w), F32),
                pltpu.VMEM((L, hd), BF16),
                pltpu.VMEM((1, L), jnp.int32),
                pltpu.VMEM(scales.shape, BF16),
                pltpu.VMEM((L, D), BF16),
                pltpu.VMEM((wide, hd), BF16),
                pltpu.VMEM((wide, hd), BF16),
                pltpu.VMEM(levels.shape, BF16),
                pltpu.VMEM((n_in, 2, half_rows, hd), BF16),
                pltpu.VMEM((L, wide), F32),
                pltpu.VMEM((L, wide), BF16),
                pltpu.VMEM((L, wide), BF16),
                pltpu.VMEM((Z, Y, X, r, c_w), BF16),
                pltpu.VMEM((Z, Y, X, r, c_w), F32),
                pltpu.VMEM((Z, Y, X, r, c_w), BF16),
                pltpu.VMEM((Z, Y, X, r, c_w), BF16),
                pltpu.VMEM((Z, Y, X, r, c_w), BF16),
                pltpu.VMEM((Z, X, Y, r, c_w), BF16),
                pltpu.VMEM((Z, X, r, c_w), BF16),
                pltpu.VMEM((Z, Y, r, c_w), BF16),
                pltpu.VMEM((Z, X, r, c_w), BF16),
                pltpu.VMEM((Z, Y, r, c_w), BF16),
                pltpu.VMEM((Z, r, c_w), BF16),
                pltpu.VMEM((Z, r, c_w), BF16),
                DMA((5,)), DMA((heads,)), DMA((heads,)), DMA((4,)),
                DMA((Z,)), DMA((Z,)),
                DMA((Z, Y)), DMA((Z, Y)),
                DMA((Z, X)), DMA((Z, X)),
                DMA((Z,)), DMA((Z,)),
                DMA((Z,)), DMA((Z,)),
                DMA((Z, X)), DMA((Z, X)),
                DMA((Z, X)), DMA((Z, X)),
            ],
            compiler_params=pltpu.CompilerParams(
                collective_id=0, has_side_effects=True, vmem_limit_bytes=56 * 1024 * 1024
            ),
            cost_estimate=pl.CostEstimate(
                flops=2 * L * D * hd * 2 + 12 * heads * L * L * hd,
                bytes_accessed=8_000_000, transcendentals=heads * L * L,
            ),
        )(tokens, queries, key_rows, cotangent, segments, levels, scales)
        return pl.pallas_call(
            write_out,
            out_shape=tuple(jax.ShapeDtypeStruct(a.shape, a.dtype) for a in results),
            in_specs=[hbm] * 4,
            out_specs=(hbm,) * 4,
            scratch_shapes=[pltpu.VMEM(a.shape, a.dtype) for a in results] + [DMA((8,))],
            compiler_params=pltpu.CompilerParams(vmem_limit_bytes=56 * 1024 * 1024),
        )(*results)

    three = P(("grp", "in"), None, None)
    return jax.shard_map(
        step,
        mesh=mesh,
        in_specs=(three, three, three, three, P(("grp", "in"), None), P("in", None, None), P("in", None)),
        out_specs=(three, three, three, P("grp", "in")),
        check_vma=False,
    )
```

```python
import functools
import math

import jax
import jax.numpy as jnp
from jax import lax
from jax.experimental import pallas as pl
from jax.experimental.pallas import tpu as pltpu
from jax.sharding import PartitionSpec as P

MESH = pl.DeviceIdType.MESH
F32 = jnp.float32
BF16 = jnp.bfloat16


def dot(a, b, ca, cb):
    return lax.dot_general(a, b, (((ca,), (cb,)), ((), ())), preferred_element_type=F32)


def remote(src, dst, send, recv, dev):
    return pltpu.make_async_remote_copy(
        src_ref=src, dst_ref=dst, send_sem=send, recv_sem=recv, device_id=dev, device_id_type=MESH
    )


def kernel(
    dims,
    tok_hbm, q_hbm, k_hbm, cot_hbm, seg_hbm, lev_hbm, sca_hbm,
    att_hbm, qg_hbm, kg_hbm, wg_hbm,
    att_v, qg_v, kg_v, wg_v, key_v, seg_v, sca_v, tok, qs, cs, lev, wbuf, probs, probs_low, sg_low,
    term_send, term_own, term_recv, sum_core,
    ya_recv, xb_recv, sum_a, sum_b, xa_recv, yb_recv, sum_z, z_recv,
    in_sem, q_sem, c_sem, out_sem,
    core_s, core_r, ys_s, ys_r, xs_s, xs_r, zs_s, zs_r,
    gz_s, gz_r, gx_s, gx_r, gc_s, gc_r,
):
    Y, X, Z, heads, L, hd = dims
    r, c_w = wg_v.shape
    g, i = lax.axis_index("grp"), lax.axis_index("in")
    y, c = g // 2, lax.rem(g, 2)
    z, x = i // X, lax.rem(i, X)
    other = 1 - c
    core_dev = (y * 2 + other, i)

    def y_dev(d):
        return (lax.rem(y + d, Y) * 2 + c, i)

    def x_dev(d):
        return (g, z * X + lax.rem(x + d, X))

    def z_dev(d):
        return (g, lax.rem(z + d, Z) * X + x)

    lev_cp = pltpu.make_async_copy(lev_hbm, lev, in_sem.at[0])
    lev_cp.start()
    sca_cp = pltpu.make_async_copy(sca_hbm, sca_v, in_sem.at[2])
    sca_cp.start()
    key_cp = pltpu.make_async_copy(k_hbm.at[0], key_v, in_sem.at[3])
    key_cp.start()
    seg_cp = pltpu.make_async_copy(seg_hbm, seg_v, in_sem.at[4])
    seg_cp.start()
    q_cps, c_cps = [], []
    for h in range(heads):
        q_cps.append(pltpu.make_async_copy(
            q_hbm.at[0, :, pl.ds(h * hd, hd)], qs.at[pl.ds(h * L, L)], q_sem.at[h]))
        q_cps[-1].start()
    for h in range(heads):
        c_cps.append(pltpu.make_async_copy(
            cot_hbm.at[0, :, pl.ds(h * hd, hd)], cs.at[pl.ds(h * L, L)], c_sem.at[h]))
        c_cps[-1].start()
    tok_cp = pltpu.make_async_copy(tok_hbm.at[0], tok, in_sem.at[1])
    tok_cp.start()

    barrier = pltpu.get_barrier_semaphore()
    peers = [core_dev]
    peers += [y_dev(d) for d in range(1, Y)]
    peers += [x_dev(d) for d in range(1, X)]
    peers += [z_dev(d) for d in range(1, Z)]
    for dev in peers:
        pl.semaphore_signal(barrier, inc=1, device_id=dev, device_id_type=MESH)

    lev_cp.wait()
    blocks, block_rows = lev.shape[0], lev.shape[1]
    sca_cp.wait()
    sca = sca_v[...].astype(F32)
    if blocks > 1:
        hb = blocks // 2
        s_half = jnp.where(c == 0, sca[:hb], sca[hb:])
        own_w = lev[pl.ds(c * hb, hb)].astype(F32) * s_half[:, None, :]
        own_w = own_w.reshape(hb * block_rows, hd)
    else:
        hr = block_rows // 2
        own_w = lev[0, pl.ds(pl.multiple_of(c * hr, hr), hr)].astype(F32) * sca
    wbuf[i, c] = own_w.astype(BF16)

    pl.semaphore_wait(barrier, len(peers))

    sends = []
    outs = []

    def out(src, dst, k):
        outs.append(pltpu.make_async_copy(src, dst, out_sem.at[k]))
        outs[-1].start()

    def start(cp):
        cp.start()
        sends.append(cp)

    def piece(d, e):
        return lax.rem(z + Z - d, Z) * X + lax.rem(x + X - e, X)

    def forward_core(d, e):
        p = piece(d, e)
        start(remote(wbuf.at[p, c], wbuf.at[p, c], gc_s.at[d, e], gc_r.at[d, e], core_dev))

    def forward_x(d):
        p = piece(d, 0)
        for e in range(1, X):
            start(remote(wbuf.at[p, c], wbuf.at[p, c], gx_s.at[d, e], gx_r.at[d, e], x_dev(e)))

    def wait_z(d):
        p = piece(d, 0)
        remote(wbuf.at[p, c], wbuf.at[p, c], gz_s.at[d], gz_r.at[d], z_dev(d)).wait_recv()

    def wait_x(d, e):
        p = piece(d, e)
        remote(wbuf.at[p, c], wbuf.at[p, c], gx_s.at[d, e], gx_r.at[d, e], x_dev(e)).wait_recv()

    def wait_core(d, e):
        p = piece(d, e)
        remote(wbuf.at[p, other], wbuf.at[p, other], gc_s.at[d, e], gc_r.at[d, e], core_dev).wait_recv()

    for d in range(1, Z):
        start(remote(wbuf.at[i, c], wbuf.at[i, c], gz_s.at[d], gz_r.at[d], z_dev(d)))
    forward_x(0)
    forward_core(0, 0)

    wide = heads * L
    factor = hd ** -0.5
    key_cp.wait()
    seg_cp.wait()
    keys = key_v[...]
    lane = lax.broadcasted_iota(jnp.int32, (1, wide), 1)
    s_pos = lane
    for h in range(1, heads):
        s_pos = jnp.where(lane >= h * L, lane - h * L, s_pos)
    t_pos = lax.broadcasted_iota(jnp.int32, (L, 1), 0)
    seg_row = seg_v[...].astype(F32)
    sq_r = lax.broadcasted_iota(jnp.int32, (L, L), 0)
    sq_c = lax.broadcasted_iota(jnp.int32, (L, L), 1)
    seg_col = jnp.sum(jnp.where(sq_r == sq_c, seg_row, 0.0), axis=1, keepdims=True)
    seg_wide = jnp.sum(jnp.where(t_pos == s_pos, seg_col, 0.0), axis=0, keepdims=True)
    allowed = (t_pos <= s_pos) & (seg_col == seg_wide)
    for cp in q_cps:
        cp.wait()
    scores = jnp.where(allowed, dot(keys, qs[...], 1, 1) * factor, -jnp.inf)
    expo = jnp.exp(scores - jnp.max(scores, axis=0, keepdims=True))
    pr = expo * (1.0 / jnp.sum(expo, axis=0, keepdims=True))
    probs[...] = pr
    probs_low[...] = pr.astype(BF16)
    for cp in c_cps:
        cp.wait()
    vg = dot(probs_low[...], cs[...], 1, 0).astype(BF16).astype(F32)
    vg_t = vg.T.reshape(Y, 2, r, L)
    mine = jnp.where(c == 0, vg_t[:, 0], vg_t[:, 1]).reshape(Y * r, L)
    theirs = jnp.where(c == 0, vg_t[:, 1], vg_t[:, 0]).reshape(Y * r, L)
    vg_rows = jnp.concatenate([theirs, mine], axis=0).astype(BF16)

    tok_cp.wait()
    half = Y * r
    z_half = (Z + 1) // 2
    order = [zz for k in range(z_half) for zz in (k, k + z_half) if zz < Z]

    def y_copy(zz, d):
        if zz < z_half:
            src, dst = sum_core.at[zz, lax.rem(y + d, Y)], ya_recv.at[zz, d]
        else:
            src, dst = sum_b.at[zz, lax.rem(y + d, Y)], yb_recv.at[zz, d]
        return remote(src, dst, ys_s.at[zz, d], ys_r.at[zz, d], y_dev(d))

    def x_copy(zz, d):
        if zz < z_half:
            src, dst = sum_a.at[zz, lax.rem(x + d, X)], xa_recv.at[zz, d]
        else:
            src, dst = sum_core.at[zz, :, lax.rem(x + d, X)], xb_recv.at[zz, d]
        return remote(src, dst, xs_s.at[zz, d], xs_r.at[zz, d], x_dev(d))

    def core_copy(zz):
        return remote(term_send.at[zz], term_recv.at[zz], core_s.at[zz], core_r.at[zz], core_dev)

    def join_cores(zz):
        core_copy(zz).wait_recv()
        sum_core[zz] = (term_own[zz] + term_recv[zz].astype(F32)).astype(BF16)
        for d in range(1, Y if zz < z_half else X):
            start(y_copy(zz, d) if zz < z_half else x_copy(zz, d))

    before = None
    for zz in order:
        for xx in range(X):
            at = (zz * X + xx) * c_w
            t = dot(vg_rows, tok[:, at:at + c_w], 1, 0)
            term_send[zz, :, xx] = t[:half].reshape(Y, r, c_w).astype(BF16)
            term_own[zz, :, xx] = t[half:].reshape(Y, r, c_w)
        start(core_copy(zz))
        if before is not None:
            join_cores(before)
        before = zz
    join_cores(before)

    gathered = 0
    for zz in order:
        if zz < z_half:
            total = sum_core[zz, y].astype(F32)
            for d in range(1, Y):
                y_copy(zz, d).wait_recv()
                total = total + ya_recv[zz, d].astype(F32)
            sum_a[zz] = total.astype(BF16)
            for d in range(1, X):
                start(x_copy(zz, d))
        else:
            total = sum_core[zz, :, x].astype(F32)
            for d in range(1, X):
                x_copy(zz, d).wait_recv()
                total = total + xb_recv[zz, d].astype(F32)
            sum_b[zz] = total.astype(BF16)
            for d in range(1, Y):
                start(y_copy(zz, d))
        gathered += 1
        if gathered < Z:
            wait_z(gathered)
            forward_x(gathered)
            forward_core(gathered, 0)

    for zz in order:
        if zz < z_half:
            total = sum_a[zz, x].astype(F32)
            for d in range(1, X):
                x_copy(zz, d).wait_recv()
                total = total + xa_recv[zz, d].astype(F32)
        else:
            total = sum_b[zz, y].astype(F32)
            for d in range(1, Y):
                y_copy(zz, d).wait_recv()
                total = total + yb_recv[zz, d].astype(F32)
        sum_z[zz] = total.astype(BF16)

        @pl.when(z != zz)
        def _():
            d = lax.rem(zz + Z - z, Z)
            remote(sum_z.at[zz], z_recv.at[d], zs_s.at[d], zs_r.at[d], z_dev(d)).start()

    values = jnp.zeros((L, hd), F32)
    piece_rows = 2 * wbuf.shape[2]
    for d in range(Z):
        for e in range(1, X):
            wait_x(d, e)
            forward_core(d, e)
        if d:
            for e in range(X):
                wait_core(d - 1, e)
                p = piece(d - 1, e)
                cols = pl.ds(pl.multiple_of(p * piece_rows, 128), piece_rows)
                values = values + dot(tok[:, cols], wbuf[p].reshape(piece_rows, hd), 1, 0)
    for e in range(X):
        wait_core(Z - 1, e)
        p = piece(Z - 1, e)
        cols = pl.ds(pl.multiple_of(p * piece_rows, 128), piece_rows)
        values = values + dot(tok[:, cols], wbuf[p].reshape(piece_rows, hd), 1, 0)
    v_low = values.astype(BF16)

    att = dot(probs_low[...], v_low, 0, 0).astype(BF16)
    for h in range(heads):
        att_v[:, h * hd:(h + 1) * hd] = att[h * L:(h + 1) * L]
    out(att_v, att_hbm.at[0], 0)
    pg = dot(v_low, cs[...], 1, 1)
    weighted = probs[...] * pg
    centre = jnp.sum(weighted, axis=0, keepdims=True)
    sg_low[...] = ((weighted - probs[...] * centre) * factor).astype(BF16)
    qg = dot(sg_low[...], keys, 0, 0).astype(BF16)
    for h in range(heads):
        qg_v[:, h * hd:(h + 1) * hd] = qg[h * L:(h + 1) * L]
    out(qg_v, qg_hbm.at[0], 1)
    kg_v[...] = dot(sg_low[...], qs[...], 1, 0).astype(BF16)
    out(kg_v, kg_hbm.at[0], 2)

    total = sum_z[z].astype(F32)
    for d in range(1, Z):
        remote(z_recv.at[d], z_recv.at[d], zs_s.at[d], zs_r.at[d], z_dev(d)).wait_recv()
        total = total + z_recv[d].astype(F32)
    wg_v[...] = total * (1.0 / (2 * Y * X * Z))
    out(wg_v, wg_hbm, 3)
    for cp in sends:
        cp.wait_send()
    for d in range(1, Z):
        remote(sum_z.at[0], z_recv.at[d], zs_s.at[d], zs_r.at[d], z_dev(d)).wait_send()
    for cp in outs:
        cp.wait()


def write_out(*refs):
    held, sems = refs[8:12], refs[12]
    into = [pltpu.make_async_copy(refs[k], held[k], sems.at[k]) for k in range(4)]
    away = [pltpu.make_async_copy(held[k], refs[4 + k], sems.at[4 + k]) for k in range(4)]
    for cp in into:
        cp.start()
    for a, b in zip(into, away):
        a.wait()
        b.start()
    for cp in away:
        cp.wait()


def solution(mesh):
    n_grp, n_in = mesh.shape["grp"], mesh.shape["in"]
    Y = n_grp // 2
    X = 2 ** (int(math.log2(n_in)) // 3)
    Z = n_in // X

    def step(tokens, queries, key_rows, cotangent, segments, levels, scales):
        _, L, D = tokens.shape
        hd = key_rows.shape[2]
        heads = queries.shape[2] // hd
        wide = heads * L
        r, c_w = hd // n_grp, D // n_in
        half_rows = c_w // 2
        hbm = pl.BlockSpec(memory_space=pltpu.HBM)
        DMA = pltpu.SemaphoreType.DMA
        results = pl.pallas_call(
            functools.partial(kernel, (Y, X, Z, heads, L, hd)),
            out_shape=(
                jax.ShapeDtypeStruct(queries.shape, BF16),
                jax.ShapeDtypeStruct(queries.shape, BF16),
                jax.ShapeDtypeStruct(key_rows.shape, BF16),
                jax.ShapeDtypeStruct((r, c_w), F32),
            ),
            in_specs=[hbm] * 7,
            out_specs=(hbm,) * 4,
            scratch_shapes=[
                pltpu.VMEM((L, heads * hd), BF16),
                pltpu.VMEM((L, heads * hd), BF16),
                pltpu.VMEM((L, hd), BF16),
                pltpu.VMEM((r, c_w), F32),
                pltpu.VMEM((L, hd), BF16),
                pltpu.VMEM((1, L), jnp.int32),
                pltpu.VMEM(scales.shape, BF16),
                pltpu.VMEM((L, D), BF16),
                pltpu.VMEM((wide, hd), BF16),
                pltpu.VMEM((wide, hd), BF16),
                pltpu.VMEM(levels.shape, BF16),
                pltpu.VMEM((n_in, 2, half_rows, hd), BF16),
                pltpu.VMEM((L, wide), F32),
                pltpu.VMEM((L, wide), BF16),
                pltpu.VMEM((L, wide), BF16),
                pltpu.VMEM((Z, Y, X, r, c_w), BF16),
                pltpu.VMEM((Z, Y, X, r, c_w), F32),
                pltpu.VMEM((Z, Y, X, r, c_w), BF16),
                pltpu.VMEM((Z, Y, X, r, c_w), BF16),
                pltpu.VMEM((Z, Y, X, r, c_w), BF16),
                pltpu.VMEM((Z, X, Y, r, c_w), BF16),
                pltpu.VMEM((Z, X, r, c_w), BF16),
                pltpu.VMEM((Z, Y, r, c_w), BF16),
                pltpu.VMEM((Z, X, r, c_w), BF16),
                pltpu.VMEM((Z, Y, r, c_w), BF16),
                pltpu.VMEM((Z, r, c_w), BF16),
                pltpu.VMEM((Z, r, c_w), BF16),
                DMA((5,)), DMA((heads,)), DMA((heads,)), DMA((4,)),
                DMA((Z,)), DMA((Z,)),
                DMA((Z, Y)), DMA((Z, Y)),
                DMA((Z, X)), DMA((Z, X)),
                DMA((Z,)), DMA((Z,)),
                DMA((Z,)), DMA((Z,)),
                DMA((Z, X)), DMA((Z, X)),
                DMA((Z, X)), DMA((Z, X)),
            ],
            compiler_params=pltpu.CompilerParams(
                collective_id=0, has_side_effects=True, vmem_limit_bytes=56 * 1024 * 1024
            ),
            cost_estimate=pl.CostEstimate(
                flops=2 * L * D * hd * 2 + 12 * heads * L * L * hd,
                bytes_accessed=8_000_000, transcendentals=heads * L * L,
            ),
        )(tokens, queries, key_rows, cotangent, segments, levels, scales)
        return pl.pallas_call(
            write_out,
            out_shape=tuple(jax.ShapeDtypeStruct(a.shape, a.dtype) for a in results),
            in_specs=[hbm] * 4,
            out_specs=(hbm,) * 4,
            scratch_shapes=[pltpu.VMEM(a.shape, a.dtype) for a in results] + [DMA((8,))],
            compiler_params=pltpu.CompilerParams(vmem_limit_bytes=56 * 1024 * 1024),
        )(*results)

    three = P(("grp", "in"), None, None)
    return jax.shard_map(
        step,
        mesh=mesh,
        in_specs=(three, three, three, three, P(("grp", "in"), None), P("in", None, None), P("in", None)),
        out_specs=(three, three, three, P("grp", "in")),
        check_vma=False,
    )
```
